256 devices in a mesh: leaf: 32 (over z, y), panel: 8 (over x, core).
Axes of the slice: x: 4, y: 4, z: 8, core: 2. Of those that a mesh axis runs over, the one named last changes fastest.
Arguments:
- interface_block: float32 [32, 2048, 2048], P('leaf', 'panel'), may hold values from -0.125 to 0.125
- coupling: bfloat16 [32, 2048, 128], P('leaf', 'panel'), may hold values from -0.375 to 0.375
- eigenvalues: float32 [32, 128], P('leaf'), may hold values from 0.5 to 8
- mode_counts: int32 [32], P('leaf'), may hold values from 64 to 128, as said below
- interface_coords: bfloat16 [32, 2048, 1024], P('leaf', 'panel'), may hold values from -6 to 6
- modal_coords: bfloat16 [32, 128, 4096], P('leaf'), may hold values from -6 to 6
Outputs:
- mode_shapes: float32 [32, 2048, 1024], P('leaf', 'panel')
The draws below stay inside these ranges and needn't reach their ends.
Inputs may be any that keep to these rules, and one draw needn't show every extreme that they name: `mode_counts`: modes kept by each substructure; some substructure keeps all 128.
All inputs are finite; a program needn't handle non-finite values.
Results may differ from the reference program's by a relative error of at most 0.0023.
Values may be sent and summed in bfloat16 or wider, within the bound.
A program may use at most 128 MiB of HBM per device.

```python
import math
import jax
import jax.numpy as jnp
from jax import lax

NI = 2048
M = 128
RL = 1024
LEAVES = 32
GROUP = 4


def draw_mode_counts(key, part):
    first, second = jax.random.split(key)
    counts = jax.random.randint(first, (LEAVES,), M // 2, M + 1)
    where = jax.random.randint(second, (), 0, LEAVES)
    return counts.at[where].set(M).astype(jnp.int32)


def block_levels(rng, extent, cuts, low, top_value):
    factor_of, own = 1.0, jax.random.fold_in(rng, 6)
    for axis_at, shards_of in cuts:
        draws = jnp.exp(jax.random.uniform(jax.random.fold_in(own, axis_at), (shards_of,), jnp.float32, low / len(cuts), top_value / len(cuts)))
        factor_of = factor_of * jnp.repeat(draws, extent[axis_at] // shards_of).reshape([-1 if axis == axis_at else 1 for axis in range(len(extent))])
    return factor_of


def normal_values(own_key, dims, spread, most, cuts=(), kind=jnp.bfloat16):
    factor_of = block_levels(own_key, dims, cuts, -0.22, 0.18) if cuts else 1.0
    array = jax.random.normal(own_key, dims, jnp.float32) * spread * factor_of
    return jnp.minimum(jnp.maximum(array, -most), most).astype(kind)


def setup_inputs(seed: int = 0) -> dict:
    key_list = jax.random.split(jax.random.key(seed), 7)
    return {
        "interface_block": normal_values(key_list[0], (LEAVES, NI, NI), NI ** -0.5, 0.125, ((0, 32), (1, 8)), jnp.float32),
        "coupling": normal_values(key_list[1], (LEAVES, NI, M), (2 * M) ** -0.5, 0.375, ((0, 32), (1, 8))),
        "eigenvalues": jnp.clip(jnp.exp(math.log(8.0) - 2.7725887 * jax.random.uniform(key_list[2], (LEAVES, M), jnp.float32) ** block_levels(key_list[2], (LEAVES, M), ((0, 32),), -0.2, 0.2)), 0.5, 8.0),
        "mode_counts": draw_mode_counts(jax.random.fold_in(key_list[6], 71), 0),
        "interface_coords": normal_values(key_list[4], (LEAVES, NI, RL), 1.0, 6.0, ((0, 32), (1, 8))),
        "modal_coords": normal_values(key_list[5], (LEAVES, M, GROUP * RL), 1.0, 6.0, ((0, 32),)),
    }


def group_shapes(packed):
    block4, coup4, lam4, count4, coords4, modal4 = packed
    index = jnp.arange(M, dtype=jnp.int32)
    mask = (index[None, :] < count4[:, None]).astype(jnp.float32)
    scaled = (coup4.astype(jnp.float32) * (mask / lam4)[:, None, :]).astype(jnp.bfloat16)
    product = jnp.einsum("lim,ljm->lij", scaled.astype(jnp.float32), coup4.astype(jnp.float32))
    merged = jnp.sum(block4 - product, axis=0)
    modal_term = jnp.einsum("lik,lkc->ic", scaled.astype(jnp.float32), modal4.astype(jnp.float32))
    modal_term = jnp.transpose(modal_term.reshape(NI, GROUP, RL), (1, 0, 2))
    shapes = jnp.einsum("ij,ljr->lir", merged, coords4.astype(jnp.float32), precision=lax.Precision.HIGHEST)
    return shapes + modal_term


def reference(interface_block, coupling, eigenvalues, mode_counts, interface_coords, modal_coords):
    groups = LEAVES // GROUP
    packed = (interface_block.reshape(groups, GROUP, NI, NI),
              coupling.reshape(groups, GROUP, NI, M),
              eigenvalues.reshape(groups, GROUP, M),
              mode_counts.reshape(groups, GROUP),
              interface_coords.reshape(groups, GROUP, NI, RL),
              modal_coords.reshape(groups, GROUP, M, GROUP * RL))
    result = lax.map(group_shapes, packed)
    return result.reshape(LEAVES, NI, RL)
```

```python
import jax
import jax.numpy as jnp
from jax import lax
from jax.experimental import pallas as pl
from jax.experimental.pallas import tpu as pltpu
from jax.sharding import PartitionSpec as P

MESH = pl.DeviceIdType.MESH
BF, F32 = jnp.bfloat16, jnp.float32
G = 4
ROWS, NI, M, RL = 256, 2048, 128, 1024
BLK, SUB = 512, 128
QR = 16
COPIES = 80


def kernel(a_hbm, c_hbm, lam_ref, cnt_ref, x_hbm, q_hbm, out_ref,
           abuf, call, sg, qg, xall, rs, rr, mg, mo, ml, ssem, rsem, lsem):
    leaf, panel = lax.axis_index("leaf"), lax.axis_index("panel")
    y, x, core = lax.rem(leaf, G), panel // 2, lax.rem(panel, 2)
    base = leaf - y

    def wrap(v):
        return lax.rem(v + G, G)

    def at_y(d):
        return {"leaf": base + wrap(y + d), "panel": panel}

    def at_x(d):
        return {"leaf": leaf, "panel": wrap(x + d) * 2 + core}

    sibling = {"leaf": leaf, "panel": x * 2 + 1 - core}
    partners = [sibling] + [at_y(d) for d in (1, -1, 2)] + [at_x(d) for d in (1, -1, 2)]

    used = []

    def remote(src, dst, device):
        n = len(used)
        copy = pltpu.make_async_remote_copy(
            src_ref=src, dst_ref=dst, send_sem=ssem.at[n], recv_sem=rsem.at[n],
            device_id=device, device_id_type=MESH)
        copy.start()
        used.append(copy)
        return copy

    def rows_of(d, c=None):
        return pl.multiple_of((wrap(x + d) * 2 + (core if c is None else c)) * ROWS, ROWS)

    def block_rows(d):
        return pl.multiple_of(wrap(x + d) * BLK, BLK)

    order = (0, -1, 1, 2)
    mine = rows_of(0)
    qrow = pl.multiple_of(panel * QR, QR)

    local = [pltpu.make_async_copy(c_hbm.at[0], call.at[pl.ds(mine, ROWS)], lsem.at[0])]
    for j, d in enumerate(order):
        local.append(pltpu.make_async_copy(a_hbm.at[0, :, pl.ds(block_rows(d), BLK)], abuf.at[j], lsem.at[1 + j]))
    local.append(pltpu.make_async_copy(x_hbm.at[0], xall.at[pl.ds(mine, ROWS)], lsem.at[5]))
    local.append(pltpu.make_async_copy(q_hbm.at[0, :, pl.ds(pl.multiple_of(y * RL, RL), RL)], qg.at[0], lsem.at[6]))
    for copy in local:
        copy.start()

    barrier = pltpu.get_barrier_semaphore()
    for device in partners:
        pl.semaphore_signal(barrier, inc=1, device_id=device, device_id_type=MESH)
    pl.semaphore_wait(barrier, len(partners))

    c_sib = remote(c_hbm.at[0], call.at[pl.ds(mine, ROWS)], sibling)
    c_in = {}
    for d in (1, -1, 2):
        c_in[-d if d != 2 else 2] = remote(c_hbm.at[0], call.at[pl.ds(mine, ROWS)], at_x(d))
    q_in = []
    for d in (1, -1, 2):
        slot = (G - d) % G
        q_in.append(remote(
            q_hbm.at[0, pl.ds(qrow, QR), pl.ds(pl.multiple_of(wrap(y + d) * RL, RL), RL)],
            qg.at[slot, pl.ds(qrow, QR)], at_y(d)))
    H = ROWS // 2
    x_in = {}

    def x_half(h):
        return x_hbm.at[0, pl.ds(h * H, H)]

    for d, h in ((1, 0), (-1, 1), (1, 1), (-1, 0)):
        x_in[-d, h] = remote(x_half(h), xall.at[pl.ds(mine + h * H, H)], at_x(d))
    x_sib = remote(x_hbm.at[0], xall.at[pl.ds(mine, ROWS)], sibling)

    local[0].wait()
    keep = (lax.broadcasted_iota(jnp.int32, (1, M), 1) < cnt_ref[0]).astype(F32)
    scale = keep / lam_ref[...]
    sg[0] = (call[pl.ds(mine, ROWS), :].astype(F32) * scale).astype(BF)
    s_in = []
    for d in (1, -1, 2):
        s_in.append(remote(sg.at[0], sg.at[(G - d) % G], at_y(d)))

    r_in = []

    def schur(j):
        local[1 + j].wait()
        got = []
        for d in (1, 3, 2, 0):
            col = pl.multiple_of(wrap(y + d) * SUB, SUB)
            ck = call[pl.ds(pl.multiple_of(block_rows(order[j]) + col, SUB), SUB), :]
            val = abuf[j, :, pl.ds(col, SUB)] - lax.dot_general(
                sg[0], ck, (((1,), (1,)), ((), ())), preferred_element_type=F32)
            if d == 0:
                mo[j] = val
            else:
                rs[j, d - 1] = val.astype(BF)
                got.append(remote(rs.at[j, d - 1], rr.at[j, G - d - 1], at_y(d)))
        r_in.append(got)

    c_sib.wait_recv()
    schur(0)
    c_fwd = {}
    for d in (-1, 1, 2):
        c_in[d].wait_recv()
        r = rows_of(d)
        c_fwd[d] = remote(call.at[pl.ds(r, ROWS)], call.at[pl.ds(r, ROWS)], sibling)
    for j in (1, 2, 3):
        c_fwd[order[j]].wait_recv()
        schur(j)

    for copy in q_in:
        copy.wait_recv()

    def q_piece(d):
        return qg.at[pl.ds(1, 3), pl.ds(pl.multiple_of((wrap(x + d) * 2 + core) * QR, QR), QR)]

    qx_in = {}
    for d in (1, -1, 2):
        qx_in[-d if d != 2 else 2] = remote(q_piece(0), q_piece(0), at_x(d))
    q_sib = [remote(q_piece(0), q_piece(0), sibling)]

    m_in = []

    def reduce(j):
        for copy in r_in[j]:
            copy.wait_recv()
        total = mo[j] + rr[j, 0].astype(F32) + rr[j, 1].astype(F32) + rr[j, 2].astype(F32)
        high = total.astype(BF)
        mg[j, y] = high
        ml[j] = (total - high.astype(F32)).astype(BF)
        m_in.append([remote(mg.at[j, y], mg.at[j, y], at_y(1)), remote(mg.at[j, y], mg.at[j, y], at_y(-1))])

    m_fwd = []

    def forward_m(j):
        fwd = []
        for n, (d, h) in enumerate(((-1, 0), (1, 1))):
            m_in[j][n].wait_recv()
            piece = mg.at[j, wrap(y + d), pl.ds(h * H, H)]
            fwd.append(remote(piece, piece, at_y(-d)))
        m_fwd.append(fwd)

    x_fwd = []
    x_share = {}

    def share(d, h):
        piece = xall.at[pl.ds(rows_of(d) + h * H, H)]
        x_share[d, h] = remote(piece, piece, sibling)

    reduce(0)
    reduce(1)
    for d, h in ((-1, 0), (1, 1)):
        x_in[d, h].wait_recv()
        piece = xall.at[pl.ds(rows_of(d) + h * H, H)]
        x_fwd.append(remote(piece, piece, at_x(-d)))
        share(d, h)
    forward_m(0)
    reduce(2)
    forward_m(1)
    for d in (-1, 1, 2):
        qx_in[d].wait_recv()
        q_sib.append(remote(q_piece(d), q_piece(d), sibling))
    reduce(3)
    for d, h in ((-1, 1), (1, 0)):
        x_in[d, h].wait_recv()
        share(d, h)
    forward_m(2)

    for copy in s_in + q_sib:
        copy.wait_recv()
    local[6].wait()
    scaled = jnp.concatenate([sg[i] for i in range(G)], axis=1)
    out_ref[0] = jnp.dot(scaled, qg[...].reshape(G * M, RL), preferred_element_type=F32)

    def product(j):
        k = block_rows(order[j])
        merged = jnp.concatenate([mg[j, o] for o in range(G)], axis=1)
        out_ref[0] += jnp.dot(merged, xall[pl.ds(k, BLK), :], preferred_element_type=F32)
        own = pl.multiple_of(k + y * SUB, SUB)
        out_ref[0] += jnp.dot(ml[j], xall[pl.ds(own, SUB), :], preferred_element_type=F32)

    def ready(j):
        for copy in m_fwd[j]:
            copy.wait_recv()

    x_sib.wait_recv()
    local[5].wait()
    ready(0)
    product(0)
    forward_m(3)
    for h, copy in enumerate(x_fwd):
        copy.wait_recv()
        share(2, h)
    for j in (1, 2, 3):
        ready(j)
        for h in (0, 1):
            x_share[order[j], h].wait_recv()
        product(j)
    for copy in used:
        copy.wait_send()


def on_device(interface_block, coupling, eigenvalues, mode_counts, interface_coords, modal_coords):
    anywhere = pl.BlockSpec(memory_space=pl.ANY)
    vmem = pl.BlockSpec(memory_space=pltpu.VMEM)
    return pl.pallas_call(
        kernel,
        name="merge_recover",
        out_shape=jax.ShapeDtypeStruct((1, ROWS, RL), F32),
        in_specs=[anywhere, anywhere, vmem, pl.BlockSpec(memory_space=pltpu.SMEM), anywhere, anywhere],
        out_specs=vmem,
        scratch_shapes=[
            pltpu.VMEM((G, ROWS, BLK), F32),
            pltpu.VMEM((NI, M), BF),
            pltpu.VMEM((G, ROWS, M), BF),
            pltpu.VMEM((G, M, RL), BF),
            pltpu.VMEM((NI, RL), BF),
            pltpu.VMEM((G, G - 1, ROWS, SUB), BF),
            pltpu.VMEM((G, G - 1, ROWS, SUB), BF),
            pltpu.VMEM((G, G, ROWS, SUB), BF),
            pltpu.VMEM((G, ROWS, SUB), F32),
            pltpu.VMEM((G, ROWS, SUB), BF),
            pltpu.SemaphoreType.DMA((COPIES,)),
            pltpu.SemaphoreType.DMA((COPIES,)),
            pltpu.SemaphoreType.DMA((7,)),
        ],
        compiler_params=pltpu.CompilerParams(
            collective_id=0, has_side_effects=True, vmem_limit_bytes=40 * 2**20),
        cost_estimate=pl.CostEstimate(flops=1_500_000_000, bytes_accessed=5 * 2**20, transcendentals=0),
    )(interface_block, coupling, eigenvalues, mode_counts, interface_coords, modal_coords)


def solution(mesh):
    placed = (
        P("leaf", "panel", None),
        P("leaf", "panel", None),
        P("leaf", None),
        P("leaf"),
        P("leaf", "panel", None),
        P("leaf", None, None),
    )
    return jax.shard_map(
        on_device, mesh=mesh, in_specs=placed, out_specs=P("leaf", "panel", None), check_vma=False
    )
```

```python
import functools

import jax
import jax.numpy as jnp
from jax import lax
from jax.experimental import pallas as pl
from jax.experimental.pallas import tpu as pltpu
from jax.sharding import PartitionSpec as P

MESH = pl.DeviceIdType.MESH
BF, F32 = jnp.bfloat16, jnp.float32
G = 4
ROWS, NI, M, RL = 256, 2048, 128, 1024
BLK, SUB, QTR = 512, 128, 64
QR = 16
COPIES = 90
OFFSETS = (0, -1, 1, 2)


def kernel(a_hbm, c_hbm, lam_hbm, cnt_hbm, x_hbm, q_hbm, out_ref,
           lam_ref, cnt_ref, abuf, call, sg, qg, xall, rs, rr, near, mg, mo, ml, ssem, rsem, lsem):
    leaf, panel = lax.axis_index("leaf"), lax.axis_index("panel")
    y, x, core = lax.rem(leaf, G), panel // 2, lax.rem(panel, 2)
    base = leaf - y

    def wrap(v):
        return lax.rem(v + G, G)

    def at_y(d):
        return {"leaf": base + wrap(y + d), "panel": panel}

    def at_x(d):
        return {"leaf": leaf, "panel": wrap(x + d) * 2 + core}

    sibling = {"leaf": leaf, "panel": x * 2 + 1 - core}
    partners = [sibling] + [at_y(d) for d in (1, -1, 2)] + [at_x(d) for d in (1, -1)]

    barrier = pltpu.get_barrier_semaphore()
    for device in partners:
        pl.semaphore_signal(barrier, inc=1, device_id=device, device_id_type=MESH)

    used = []

    def remote(src, dst, device):
        n = len(used)
        copy = pltpu.make_async_remote_copy(
            src_ref=src, dst_ref=dst, send_sem=ssem.at[n], recv_sem=rsem.at[n],
            device_id=device, device_id_type=MESH)
        copy.start()
        used.append(copy)
        return copy

    def c_rows(j, first=0, size=ROWS):
        return call.at[pl.ds(pl.multiple_of(j * BLK + core * ROWS + first, SUB), size)]

    def x_rows(j, q=0, n=4):
        return xall.at[pl.ds(pl.multiple_of(j * BLK + core * ROWS + q * QTR, QTR), n * QTR)]

    def q_rows(d, first=0, size=RL):
        row = pl.multiple_of((wrap(x + d) * 2 + core) * QR, QR)
        return qg.at[pl.ds(1, G - 1), pl.ds(row, QR), pl.ds(first, size)]

    local = {}

    def fetch(name, src, dst):
        local[name] = pltpu.make_async_copy(src, dst, lsem.at[len(local)])
        local[name].start()

    fetch("c", c_hbm.at[0], c_rows(0))
    fetch("lam", lam_hbm, lam_ref)
    fetch("cnt", cnt_hbm, cnt_ref)
    for j, d in enumerate(OFFSETS):
        fetch(j, a_hbm.at[0, :, pl.ds(pl.multiple_of(wrap(x + d) * BLK, BLK), BLK)], abuf.at[j])
    fetch("x", x_hbm.at[0], x_rows(0))
    fetch("q", q_hbm.at[0, :, pl.ds(pl.multiple_of(y * RL, RL), RL)], qg.at[0])

    for name in ("c", "lam", "cnt"):
        local[name].wait()
    keep = (lax.broadcasted_iota(jnp.int32, (1, M), 1) < cnt_ref[0]).astype(F32)
    scale = keep / lam_ref[...]
    mine = call[pl.ds(pl.multiple_of(core * ROWS, ROWS), ROWS), :]
    sg[0] = (mine.astype(F32) * scale).astype(BF)

    pl.semaphore_wait(barrier, len(partners))

    got = {}

    def send_coupling():
        got["c0"] = remote(c_hbm.at[0], c_rows(0), sibling)
        got["c-1"] = remote(c_hbm.at[0], c_rows(1), at_x(1))
        got["c1"] = remote(c_hbm.at[0], c_rows(2), at_x(-1))

    def send_coords(way, q):
        src = x_hbm.at[0, pl.ds(q * QTR, QTR)]
        got["x", -way, q] = remote(src, x_rows(1 if way == 1 else 2, q, 1), at_x(way))

    def forward_coords(way, q):
        got["x", -way, q].wait_recv()
        got["x", 2, q] = remote(x_rows(1 if way == 1 else 2, q, 1), x_rows(3, q, 1), at_x(way))

    def share_coords(d, q, n, waits=()):
        for i in waits:
            got["x", d, i].wait_recv()
        j = OFFSETS.index(d)
        got["xs", d, q] = remote(x_rows(j, q, n), x_rows(j, q, n), sibling)

    def share_own_coords():
        got["xs", 0, 0] = remote(x_hbm.at[0], x_rows(0), sibling)

    def send_scaled():
        for way in (1, -1):
            got["s", -way] = remote(sg.at[0], sg.at[(G - way) % G], at_y(way))

    def forward_scaled():
        for way, h in ((1, 0), (-1, 1)):
            got["s", -way].wait_recv()
            piece = pl.ds(h * SUB, SUB)
            got["sf", way] = remote(sg.at[(G - way) % G, piece], sg.at[2, piece], at_y(way))

    def send_modal(d):
        col = pl.multiple_of(wrap(y + d) * RL, RL)
        for far in (0, 2):
            row = pl.ds(pl.multiple_of((wrap(x + far) * 2 + core) * QR, QR), QR)
            got["q", d, far] = remote(q_hbm.at[0, row, pl.ds(col, RL)], qg.at[(G - d) % G, row], at_y(d))

    def share_modal(d):
        got["qs", d] = remote(q_rows(d), q_rows(d), sibling)

    def spread_modal():
        for d in (2, 1, -1):
            got["q", d, 0].wait_recv()
        for way in (1, -1):
            got["qx", -way] = remote(q_rows(0), q_rows(0), at_x(way))
        share_modal(0)
        for d in (2, 1, -1):
            got["q", d, 2].wait_recv()
        share_modal(2)

    def pass_modal():
        for d in (-1, 1):
            got["qx", d].wait_recv()
            share_modal(d)

    def spread_coupling():
        for way, h in ((1, 0), (-1, 1)):
            j = 1 if way == 1 else 2
            got["c-1" if way == 1 else "c1"].wait_recv()
            got["cs", j] = remote(c_rows(j), c_rows(j), sibling)
            got["cf", way] = remote(c_rows(j, h * SUB, SUB), c_rows(3, h * SUB, SUB), at_x(way))

    def share_coupling():
        for way in (1, -1):
            got["cf", way].wait_recv()
        got["cs", 3] = remote(c_rows(3), c_rows(3), sibling)

    def scaled_up(value):
        value = value * 2.0**20
        square = value * value
        return jnp.where(value < 0, -square * square, square * square).astype(BF)

    def scaled_back(code):
        code = code.astype(F32)
        root = jnp.sqrt(jnp.sqrt(jnp.abs(code))) * 2.0**-20
        return jnp.where(code < 0, -root, root)

    top, low = pl.ds(0, SUB), pl.ds(SUB, SUB)

    def schur(j):
        local[j].wait()
        got["c0" if j == 0 else ("cs", j)].wait_recv()
        value = {}
        for d in (2, 1, 3, 0):
            col = pl.multiple_of(wrap(y + d) * SUB, SUB)
            value[d] = abuf[j, :, pl.ds(col, SUB)] - lax.dot_general(
                sg[0], call[pl.ds(pl.multiple_of(j * BLK + col, SUB), SUB), :],
                (((1,), (1,)), ((), ())), preferred_element_type=F32)
        rs[j, 0, 0] = scaled_up(value[2][:SUB])
        rs[j, 0, 1] = scaled_up(value[1][SUB:])
        rs[j, 1, 0] = scaled_up(value[2][SUB:])
        rs[j, 1, 1] = scaled_up(value[3][:SUB])
        near[j, 0] = value[1][:SUB]
        near[j, 1] = value[3][SUB:]
        mo[j] = value[0]
        for n, way in ((0, 1), (1, -1)):
            got["r", j, n] = remote(rs.at[j, n, pl.ds(0, 2)], rr.at[j, n, pl.ds(0, 2)], at_y(way))

    def combine(j):
        for n, way in ((0, 1), (1, -1)):
            got["r", j, n].wait_recv()
            rs[j, n, 2] = scaled_up(near[j, n] + scaled_back(rr[j, n, 0]))
            got["rc", j, n] = remote(rs.at[j, n, 2], rr.at[j, n, 2], at_y(way))

    def reduce(j):
        for n in (0, 1):
            got["rc", j, n].wait_recv()
        for part, a, b in ((top, 2, 1), (low, 1, 2)):
            total = mo[j, part] + scaled_back(rr[j, 0, a]) + scaled_back(rr[j, 1, b])
            high = total.astype(BF)
            mg[j, y, part] = high
            ml[j, part] = (total - high.astype(F32)).astype(BF)
        for way in (1, -1):
            got["m", j, -way] = remote(mg.at[j, y], mg.at[j, y], at_y(way))

    def forward_merged(j):
        for way, h in ((1, 0), (-1, 1)):
            got["m", j, -way].wait_recv()
            piece = mg.at[j, wrap(y - way), pl.ds(h * SUB, SUB)]
            got["mf", j, way] = remote(piece, piece, at_y(way))

    def modal():
        local["q"].wait()
        for name in (("sf", 1), ("sf", -1), ("qs", 0), ("qs", -1), ("qs", 1), ("qs", 2)):
            got[name].wait_recv()
        scaled = jnp.concatenate([sg[i] for i in range(G)], axis=1)
        out_ref[0] = jnp.dot(scaled, qg[...].reshape(G * M, RL), preferred_element_type=F32)

    def product(j):
        for way in (1, -1):
            got["mf", j, way].wait_recv()
        if j == 0:
            local["x"].wait()
        for name in list(got):
            if name[0] == "xs" and name[1] == OFFSETS[j]:
                got[name].wait_recv()
        own = pl.ds(pl.multiple_of(j * BLK + y * SUB, SUB), SUB)
        merged = jnp.concatenate([mg[j, o] for o in range(G)] + [ml[j]], axis=1)
        coords = jnp.concatenate([xall[pl.ds(j * BLK, BLK), :], xall[own, :]], axis=0)
        out_ref[0] += jnp.dot(merged, coords, preferred_element_type=F32)

    send_coupling()
    send_coords(1, 0)
    send_coords(-1, 2)
    send_scaled()
    send_modal(2)
    send_modal(1)
    send_modal(-1)
    schur(0)
    spread_coupling()
    send_coords(1, 1)
    send_coords(-1, 3)
    send_coords(1, 2)
    send_coords(-1, 0)
    send_coords(1, 3)
    send_coords(-1, 1)
    share_own_coords()
    schur(1)
    schur(2)
    forward_scaled()
    combine(0)
    share_coupling()
    spread_modal()
    schur(3)
    combine(1)
    forward_coords(1, 0)
    forward_coords(-1, 2)
    combine(2)
    forward_coords(1, 1)
    forward_coords(-1, 3)
    combine(3)
    reduce(0)
    share_coords(-1, 0, 2)
    share_coords(1, 2, 2)
    reduce(1)
    reduce(2)
    reduce(3)
    share_coords(-1, 2, 2, (2, 3))
    share_coords(1, 0, 2, (0, 1))
    forward_merged(0)
    pass_modal()
    forward_merged(1)
    share_coords(2, 0, 1, (0,))
    share_coords(2, 2, 1, (2,))
    forward_merged(2)
    modal()
    forward_merged(3)
    product(0)
    product(1)
    product(2)
    share_coords(2, 1, 1, (1,))
    share_coords(2, 3, 1, (3,))
    product(3)
    for copy in used:
        copy.wait_send()


def on_device(interface_block, coupling, eigenvalues, mode_counts, interface_coords, modal_coords):
    held = functools.partial(pltpu.with_memory_space_constraint, memory_space=pltpu.HBM)
    hbm = pl.BlockSpec(memory_space=pltpu.HBM)
    return pl.pallas_call(
        kernel,
        name="merge_recover",
        out_shape=jax.ShapeDtypeStruct((1, ROWS, RL), F32),
        in_specs=[hbm] * 6,
        out_specs=pl.BlockSpec(memory_space=pltpu.VMEM),
        scratch_shapes=[
            pltpu.VMEM((1, M), F32),
            pltpu.SMEM((1,), jnp.int32),
            pltpu.VMEM((G, ROWS, BLK), F32),
            pltpu.VMEM((NI, M), BF),
            pltpu.VMEM((G, ROWS, M), BF),
            pltpu.VMEM((G, M, RL), BF),
            pltpu.VMEM((NI, RL), BF),
            pltpu.VMEM((G, 2, 3, SUB, SUB), BF),
            pltpu.VMEM((G, 2, 3, SUB, SUB), BF),
            pltpu.VMEM((G, 2, SUB, SUB), F32),
            pltpu.VMEM((G, G, ROWS, SUB), BF),
            pltpu.VMEM((G, ROWS, SUB), F32),
            pltpu.VMEM((G, ROWS, SUB), BF),
            pltpu.SemaphoreType.DMA((COPIES,)),
            pltpu.SemaphoreType.DMA((COPIES,)),
            pltpu.SemaphoreType.DMA((9,)),
        ],
        compiler_params=pltpu.CompilerParams(
            collective_id=0, has_side_effects=True, vmem_limit_bytes=40 * 2**20),
        cost_estimate=pl.CostEstimate(flops=1_500_000_000, bytes_accessed=5 * 2**20, transcendentals=0),
    )(held(interface_block), held(coupling), held(eigenvalues), mode_counts, held(interface_coords), held(modal_coords))


def solution(mesh):
    placed = (
        P("leaf", "panel", None),
        P("leaf", "panel", None),
        P("leaf", None),
        P("leaf"),
        P("leaf", "panel", None),
        P("leaf", None, None),
    )
    return jax.shard_map(
        on_device, mesh=mesh, in_specs=placed, out_specs=P("leaf", "panel", None), check_vma=False
    )
```

```python
import functools

import jax
import jax.numpy as jnp
from jax import lax
from jax.experimental import pallas as pl
from jax.experimental.pallas import tpu as pltpu
from jax.sharding import PartitionSpec as P

MESH = pl.DeviceIdType.MESH
BF, F32 = jnp.bfloat16, jnp.float32
G = 4
ROWS, NI, M, RL = 256, 2048, 128, 1024
BLK, SUB, QTR = 512, 128, 64
QR = 16
COPIES = 90
OFFSETS = (0, -1, 1, 2)


def kernel(a_hbm, c_hbm, lam_hbm, cnt_hbm, x_hbm, q_hbm, out_ref,
           lam_ref, cnt_ref, abuf, call, sg, qg, xall, rs, rr, near, mg, mo, ml, ssem, rsem, lsem):
    leaf, panel = lax.axis_index("leaf"), lax.axis_index("panel")
    y, x, core = lax.rem(leaf, G), panel // 2, lax.rem(panel, 2)
    base = leaf - y

    def wrap(v):
        return lax.rem(v + G, G)

    def at_y(d):
        return {"leaf": base + wrap(y + d), "panel": panel}

    def at_x(d):
        return {"leaf": leaf, "panel": wrap(x + d) * 2 + core}

    sibling = {"leaf": leaf, "panel": x * 2 + 1 - core}
    partners = [sibling] + [at_y(d) for d in (1, -1, 2)] + [at_x(d) for d in (1, -1)]

    barrier = pltpu.get_barrier_semaphore()
    for device in partners:
        pl.semaphore_signal(barrier, inc=1, device_id=device, device_id_type=MESH)

    used = []

    def remote(src, dst, device):
        n = len(used)
        copy = pltpu.make_async_remote_copy(
            src_ref=src, dst_ref=dst, send_sem=ssem.at[n], recv_sem=rsem.at[n],
            device_id=device, device_id_type=MESH)
        copy.start()
        used.append(copy)
        return copy

    def c_rows(j, first=0, size=ROWS):
        return call.at[pl.ds(pl.multiple_of(j * BLK + core * ROWS + first, SUB), size)]

    def x_rows(j, q=0, n=4):
        return xall.at[pl.ds(pl.multiple_of(j * BLK + core * ROWS + q * QTR, QTR), n * QTR)]

    def q_rows(d, first=0, size=RL):
        row = pl.multiple_of((wrap(x + d) * 2 + core) * QR, QR)
        return qg.at[pl.ds(1, G - 1), pl.ds(row, QR), pl.ds(first, size)]

    local = {}

    def fetch(name, src, dst):
        local[name] = pltpu.make_async_copy(src, dst, lsem.at[len(local)])
        local[name].start()

    fetch("c", c_hbm.at[0], c_rows(0))
    fetch("lam", lam_hbm, lam_ref)
    fetch("cnt", cnt_hbm, cnt_ref)
    for j, d in enumerate(OFFSETS):
        fetch(j, a_hbm.at[0, :, pl.ds(pl.multiple_of(wrap(x + d) * BLK, BLK), BLK)], abuf.at[j])
    fetch("x", x_hbm.at[0], x_rows(0))
    fetch("q", q_hbm.at[0, :, pl.ds(pl.multiple_of(y * RL, RL), RL)], qg.at[0])

    pl.semaphore_wait(barrier, len(partners))

    got = {}

    def send_coupling():
        got["c0"] = remote(c_hbm.at[0], c_rows(0), sibling)
        got["c-1"] = remote(c_hbm.at[0], c_rows(1), at_x(1))
        got["c1"] = remote(c_hbm.at[0], c_rows(2), at_x(-1))

    def send_coords(way, q):
        src = x_hbm.at[0, pl.ds(q * QTR, QTR)]
        got["x", -way, q] = remote(src, x_rows(1 if way == 1 else 2, q, 1), at_x(way))

    def forward_coords(way, q):
        got["x", -way, q].wait_recv()
        got["x", 2, q] = remote(x_rows(1 if way == 1 else 2, q, 1), x_rows(3, q, 1), at_x(way))

    def share_coords(d, q, n, waits=()):
        for i in waits:
            got["x", d, i].wait_recv()
        j = OFFSETS.index(d)
        got["xs", d, q] = remote(x_rows(j, q, n), x_rows(j, q, n), sibling)

    def share_own_coords():
        got["xs", 0, 0] = remote(x_hbm.at[0], x_rows(0), sibling)

    def send_scaled():
        for name in ("c", "lam", "cnt"):
            local[name].wait()
        keep = (lax.broadcasted_iota(jnp.int32, (1, M), 1) < cnt_ref[0]).astype(F32)
        scale = keep / lam_ref[...]
        mine = call[pl.ds(pl.multiple_of(core * ROWS, ROWS), ROWS), :]
        sg[0] = (mine.astype(F32) * scale).astype(BF)
        for way in (1, -1):
            got["s", -way] = remote(sg.at[0], sg.at[(G - way) % G], at_y(way))

    def forward_scaled(way):
        got["s", -way].wait_recv()
        piece = pl.ds(0 if way == 1 else SUB, SUB)
        got["sf", way] = remote(sg.at[(G - way) % G, piece], sg.at[2, piece], at_y(way))

    def send_modal(d):
        col = pl.multiple_of(wrap(y + d) * RL, RL)
        for far in (0, 2):
            row = pl.ds(pl.multiple_of((wrap(x + far) * 2 + core) * QR, QR), QR)
            got["q", d, far] = remote(q_hbm.at[0, row, pl.ds(col, RL)], qg.at[(G - d) % G, row], at_y(d))

    def share_modal(d):
        got["qs", d] = remote(q_rows(d), q_rows(d), sibling)

    def spread_modal():
        for d in (2, 1, -1):
            got["q", d, 0].wait_recv()
        for way in (1, -1):
            got["qx", -way] = remote(q_rows(0), q_rows(0), at_x(way))
        share_modal(0)

    def share_far_modal():
        for d in (2, 1, -1):
            got["q", d, 2].wait_recv()
        share_modal(2)

    def pass_modal(d):
        got["qx", d].wait_recv()
        share_modal(d)

    def spread_coupling(way):
        j, h = (1, 0) if way == 1 else (2, 1)
        got["c-1" if way == 1 else "c1"].wait_recv()
        got["cs", j] = remote(c_rows(j), c_rows(j), sibling)
        got["cf", way] = remote(c_rows(j, h * SUB, SUB), c_rows(3, h * SUB, SUB), at_x(way))

    def share_coupling():
        for way in (1, -1):
            got["cf", way].wait_recv()
        got["cs", 3] = remote(c_rows(3), c_rows(3), sibling)

    def scaled_up(value):
        value = value * 2.0**20
        square = value * value
        return jnp.where(value < 0, -square * square, square * square).astype(BF)

    def scaled_back(code):
        code = code.astype(F32)
        root = jnp.sqrt(jnp.sqrt(jnp.abs(code))) * 2.0**-20
        return jnp.where(code < 0, -root, root)

    top, low = pl.ds(0, SUB), pl.ds(SUB, SUB)

    def schur(j):
        local[j].wait()
        got["c0" if j == 0 else ("cs", j)].wait_recv()
        value = {}
        for d in (2, 1, 3, 0):
            col = pl.multiple_of(wrap(y + d) * SUB, SUB)
            value[d] = abuf[j, :, pl.ds(col, SUB)] - lax.dot_general(
                sg[0], call[pl.ds(pl.multiple_of(j * BLK + col, SUB), SUB), :],
                (((1,), (1,)), ((), ())), preferred_element_type=F32)
        rs[j, 0, 0] = scaled_up(value[2][:SUB])
        rs[j, 0, 1] = scaled_up(value[1][SUB:])
        rs[j, 1, 0] = scaled_up(value[2][SUB:])
        rs[j, 1, 1] = scaled_up(value[3][:SUB])
        near[j, 0] = value[1][:SUB]
        near[j, 1] = value[3][SUB:]
        mo[j] = value[0]
        for n, way in ((0, 1), (1, -1)):
            got["r", j, n] = remote(rs.at[j, n, pl.ds(0, 2)], rr.at[j, n, pl.ds(0, 2)], at_y(way))

    def combine(j):
        for n, way in ((0, 1), (1, -1)):
            got["r", j, n].wait_recv()
            rs[j, n, 2] = scaled_up(near[j, n] + scaled_back(rr[j, n, 0]))
            got["rc", j, n] = remote(rs.at[j, n, 2], rr.at[j, n, 2], at_y(way))

    def reduce(j):
        for n in (0, 1):
            got["rc", j, n].wait_recv()
        for part, a, b in ((top, 2, 1), (low, 1, 2)):
            total = mo[j, part] + scaled_back(rr[j, 0, a]) + scaled_back(rr[j, 1, b])
            high = total.astype(BF)
            mg[j, y, part] = high
            ml[j, part] = (total - high.astype(F32)).astype(BF)
        for way in (1, -1):
            got["m", j, -way] = remote(mg.at[j, y], mg.at[j, y], at_y(way))

    def forward_merged(j, way):
        got["m", j, -way].wait_recv()
        piece = mg.at[j, wrap(y - way), top if way == 1 else low]
        got["mf", j, way] = remote(piece, piece, at_y(way))

    def modal():
        local["q"].wait()
        for name in (("sf", 1), ("sf", -1), ("qs", 0), ("qs", -1), ("qs", 1), ("qs", 2)):
            got[name].wait_recv()
        scaled = jnp.concatenate([sg[i] for i in range(G)], axis=1)
        out_ref[0] = jnp.dot(scaled, qg[...].reshape(G * M, RL), preferred_element_type=F32)

    def product(j):
        for way in (1, -1):
            got["mf", j, way].wait_recv()
        if j == 0:
            local["x"].wait()
        for name in list(got):
            if name[0] == "xs" and name[1] == OFFSETS[j]:
                got[name].wait_recv()
        own = pl.ds(pl.multiple_of(j * BLK + y * SUB, SUB), SUB)
        merged = jnp.concatenate([mg[j, o] for o in range(G)] + [ml[j]], axis=1)
        coords = jnp.concatenate([xall[pl.ds(j * BLK, BLK), :], xall[own, :]], axis=0)
        out_ref[0] += jnp.dot(merged, coords, preferred_element_type=F32)

    send_coupling()
    send_modal(2)
    send_coords(-1, 2)
    send_modal(-1)
    send_coords(1, 0)
    send_modal(1)
    send_scaled()
    schur(0)
    spread_coupling(1)
    spread_coupling(-1)
    send_coords(1, 3)
    spread_modal()
    schur(1)
    send_coords(1, 1)
    send_coords(-1, 3)
    schur(2)
    share_coupling()
    send_coords(-1, 0)
    send_coords(1, 2)
    send_coords(-1, 1)
    combine(0)
    schur(3)
    combine(1)
    combine(2)
    reduce(0)
    combine(3)
    forward_coords(1, 0)
    share_own_coords()
    forward_coords(-1, 2)
    reduce(1)
    reduce(2)
    reduce(3)
    forward_coords(1, 1)
    forward_scaled(1)
    forward_coords(-1, 3)
    forward_merged(0, 1)
    forward_scaled(-1)
    share_coords(-1, 0, 2)
    forward_merged(1, -1)
    pass_modal(1)
    forward_merged(2, 1)
    forward_merged(2, -1)
    pass_modal(-1)
    forward_merged(1, 1)
    share_coords(-1, 2, 2, (2, 3))
    share_far_modal()
    forward_merged(0, -1)
    share_coords(1, 2, 2)
    share_coords(2, 0, 1, (0,))
    share_coords(2, 2, 1, (2,))
    forward_merged(3, 1)
    forward_merged(3, -1)
    share_coords(1, 0, 2, (0, 1))
    modal()
    share_coords(2, 1, 1, (1,))
    share_coords(2, 3, 1, (3,))
    product(2)
    product(1)
    product(0)
    product(3)
    for copy in used:
        copy.wait_send()


def on_device(interface_block, coupling, eigenvalues, mode_counts, interface_coords, modal_coords):
    held = functools.partial(pltpu.with_memory_space_constraint, memory_space=pltpu.HBM)
    hbm = pl.BlockSpec(memory_space=pltpu.HBM)
    return pl.pallas_call(
        kernel,
        name="merge_recover",
        out_shape=jax.ShapeDtypeStruct((1, ROWS, RL), F32),
        in_specs=[hbm] * 6,
        out_specs=pl.BlockSpec(memory_space=pltpu.VMEM),
        scratch_shapes=[
            pltpu.VMEM((1, M), F32),
            pltpu.SMEM((1,), jnp.int32),
            pltpu.VMEM((G, ROWS, BLK), F32),
            pltpu.VMEM((NI, M), BF),
            pltpu.VMEM((G, ROWS, M), BF),
            pltpu.VMEM((G, M, RL), BF),
            pltpu.VMEM((NI, RL), BF),
            pltpu.VMEM((G, 2, 3, SUB, SUB), BF),
            pltpu.VMEM((G, 2, 3, SUB, SUB), BF),
            pltpu.VMEM((G, 2, SUB, SUB), F32),
            pltpu.VMEM((G, G, ROWS, SUB), BF),
            pltpu.VMEM((G, ROWS, SUB), F32),
            pltpu.VMEM((G, ROWS, SUB), BF),
            pltpu.SemaphoreType.DMA((COPIES,)),
            pltpu.SemaphoreType.DMA((COPIES,)),
            pltpu.SemaphoreType.DMA((9,)),
        ],
        compiler_params=pltpu.CompilerParams(
            collective_id=0, has_side_effects=True, vmem_limit_bytes=40 * 2**20),
        cost_estimate=pl.CostEstimate(flops=1_500_000_000, bytes_accessed=5 * 2**20, transcendentals=0),
    )(held(interface_block), held(coupling), held(eigenvalues), mode_counts, held(interface_coords), held(modal_coords))


def solution(mesh):
    placed = (
        P("leaf", "panel", None),
        P("leaf", "panel", None),
        P("leaf", None),
        P("leaf"),
        P("leaf", "panel", None),
        P("leaf", None, None),
    )
    return jax.shard_map(
        on_device, mesh=mesh, in_specs=placed, out_specs=P("leaf", "panel", None), check_vma=False
    )
```

```python
import functools

import jax
import jax.numpy as jnp
from jax import lax
from jax.experimental import pallas as pl
from jax.experimental.pallas import tpu as pltpu
from jax.sharding import PartitionSpec as P

MESH = pl.DeviceIdType.MESH
BF, F32 = jnp.bfloat16, jnp.float32
G = 4
ROWS, NI, M, RL = 256, 2048, 128, 1024
BLK, SUB, QTR = 512, 128, 64
QR = 16
COPIES = 90
OFFSETS = (0, -1, 1, 2)


def kernel(a_hbm, c_hbm, lam_hbm, cnt_hbm, x_hbm, q_hbm, out_ref, last_m, last_x,
           lam_ref, cnt_ref, abuf, call, sg, qg, xall, rs, rr, near, mg, mo, ml, ssem, rsem, lsem):
    leaf, panel = lax.axis_index("leaf"), lax.axis_index("panel")
    y, x, core = lax.rem(leaf, G), panel // 2, lax.rem(panel, 2)
    base = leaf - y

    def wrap(v):
        return lax.rem(v + G, G)

    def at_y(d):
        return {"leaf": base + wrap(y + d), "panel": panel}

    def at_x(d):
        return {"leaf": leaf, "panel": wrap(x + d) * 2 + core}

    sibling = {"leaf": leaf, "panel": x * 2 + 1 - core}
    partners = [sibling] + [at_y(d) for d in (1, -1, 2)] + [at_x(d) for d in (1, -1)]

    barrier = pltpu.get_barrier_semaphore()
    for device in partners:
        pl.semaphore_signal(barrier, inc=1, device_id=device, device_id_type=MESH)

    used = []

    def remote(src, dst, device):
        n = len(used)
        copy = pltpu.make_async_remote_copy(
            src_ref=src, dst_ref=dst, send_sem=ssem.at[n], recv_sem=rsem.at[n],
            device_id=device, device_id_type=MESH)
        copy.start()
        used.append(copy)
        return copy

    def c_rows(j, first=0, size=ROWS):
        return call.at[pl.ds(pl.multiple_of(j * BLK + core * ROWS + first, SUB), size)]

    def x_rows(j, q=0, n=4):
        first = 3 * BLK if j == 3 else j * BLK + core * ROWS
        return xall.at[pl.ds(pl.multiple_of(first + q * QTR, QTR), n * QTR)]

    local = {}

    def fetch(name, src, dst):
        local[name] = pltpu.make_async_copy(src, dst, lsem.at[len(local)])
        local[name].start()

    fetch("c", c_hbm.at[0], c_rows(0))
    fetch("lam", lam_hbm, lam_ref)
    fetch("cnt", cnt_hbm, cnt_ref)
    for j, d in enumerate(OFFSETS):
        fetch(j, a_hbm.at[0, :, pl.ds(pl.multiple_of(wrap(x + d) * BLK, BLK), BLK)], abuf.at[j])
    fetch("x", x_hbm.at[0], x_rows(0))
    fetch("q", q_hbm.at[0, :, pl.ds(pl.multiple_of(y * RL, RL), RL)], qg.at[0])

    pl.semaphore_wait(barrier, len(partners))

    got = {}

    def send_coupling():
        got["c0"] = remote(c_hbm.at[0], c_rows(0), sibling)
        got["c-1"] = remote(c_hbm.at[0], c_rows(1), at_x(1))
        got["c1"] = remote(c_hbm.at[0], c_rows(2), at_x(-1))

    def send_coords(way, q, n=1):
        src = x_hbm.at[0, pl.ds(q * QTR, n * QTR)]
        got["x", -way, q] = remote(src, x_rows(1 if way == 1 else 2, q, n), at_x(way))

    def forward_coords(way):
        j, q = (1, 0) if way == 1 else (2, 2)
        for i in (q, q + 1):
            got["x", -way, i].wait_recv()
        got["x", 2, q] = remote(x_rows(j, q, 2), x_rows(3, q, 2), at_x(way))

    def share_coords(d, q, wait=True):
        if wait:
            got["x", d, q].wait_recv()
        j = OFFSETS.index(d)
        there = last_x.at[pl.ds(q * QTR, 2 * QTR)] if j == 3 else x_rows(j, q, 2)
        got["xs", d, q] = remote(x_rows(j, q, 2), there, sibling)

    def share_own_coords():
        got["xs", 0, 0] = remote(x_hbm.at[0], x_rows(0), sibling)

    def send_scaled():
        for name in ("c", "lam", "cnt"):
            local[name].wait()
        keep = (lax.broadcasted_iota(jnp.int32, (1, M), 1) < cnt_ref[0]).astype(F32)
        scale = keep / lam_ref[...]
        mine = call[pl.ds(pl.multiple_of(core * ROWS, ROWS), ROWS), :]
        sg[0] = (mine.astype(F32) * scale).astype(BF)
        for way in (1, -1):
            got["s", -way] = remote(sg.at[0], sg.at[(G - way) % G], at_y(way))

    def forward_scaled(way):
        got["s", -way].wait_recv()
        piece = pl.ds(0 if way == 1 else SUB, SUB)
        got["sf", way] = remote(sg.at[(G - way) % G, piece], sg.at[2, piece], at_y(way))

    def q_rows(d, n=1):
        chip = wrap(x + d)
        first = lax.rem(chip, 2) * (M // 2) + core * (2 * QR) + (chip // 2 * QR if n == 1 else 0)
        return pl.ds(pl.multiple_of(first, QR), n * QR)

    def send_modal(d):
        col = pl.multiple_of(wrap(y + d) * RL, RL)
        got["q", d] = remote(q_hbm.at[0, q_rows(0, 2), pl.ds(col, RL)], qg.at[(G - d) % G, q_rows(0, 2)], at_y(d))

    def share_modal(d):
        piece = qg.at[pl.ds(1, G - 1), q_rows(d, 2)]
        got["qs", d] = remote(piece, piece, sibling)

    def spread_modal():
        for d in (2, 1, -1):
            got["q", d].wait_recv()
        piece = qg.at[pl.ds(1, G - 1), q_rows(0)]
        for way in (1, -1):
            got["qx", -way] = remote(piece, piece, at_x(way))
        share_modal(0)

    def pass_modal():
        for d in (-1, 1):
            got["qx", d].wait_recv()
        share_modal(1)

    def spread_coupling(way):
        j, h = (1, 0) if way == 1 else (2, 1)
        got["c-1" if way == 1 else "c1"].wait_recv()
        got["cs", j] = remote(c_rows(j), c_rows(j), sibling)
        got["cf", way] = remote(c_rows(j, h * SUB, SUB), c_rows(3, h * SUB, SUB), at_x(way))

    def share_coupling():
        for way in (1, -1):
            got["cf", way].wait_recv()
        got["cs", 3] = remote(c_rows(3), c_rows(3), sibling)

    def scaled_up(value):
        value = value * 2.0**20
        square = value * value
        return jnp.where(value < 0, -square * square, square * square).astype(BF)

    def scaled_back(code):
        code = code.astype(F32)
        root = jnp.sqrt(jnp.sqrt(jnp.abs(code))) * 2.0**-20
        return jnp.where(code < 0, -root, root)

    top, low = pl.ds(0, SUB), pl.ds(SUB, SUB)

    def schur(j):
        local[j].wait()
        got["c0" if j == 0 else ("cs", j)].wait_recv()
        value = {}
        for d in (2, 1, 3, 0):
            col = pl.multiple_of(wrap(y + d) * SUB, SUB)
            value[d] = abuf[j, :, pl.ds(col, SUB)] - lax.dot_general(
                sg[0], call[pl.ds(pl.multiple_of(j * BLK + col, SUB), SUB), :],
                (((1,), (1,)), ((), ())), preferred_element_type=F32)
        rs[j, 0, 0] = scaled_up(value[2][:SUB])
        rs[j, 0, 1] = scaled_up(value[1][SUB:])
        rs[j, 1, 0] = scaled_up(value[2][SUB:])
        rs[j, 1, 1] = scaled_up(value[3][:SUB])
        near[j, 0] = value[1][:SUB]
        near[j, 1] = value[3][SUB:]
        mo[j] = value[0]
        for n, way in ((0, 1), (1, -1)):
            got["r", j, n] = remote(rs.at[j, n, pl.ds(0, 2)], rr.at[j, n, pl.ds(0, 2)], at_y(way))

    def combine(j):
        for n, way in ((0, 1), (1, -1)):
            got["r", j, n].wait_recv()
            rs[j, n, 2] = scaled_up(near[j, n] + scaled_back(rr[j, n, 0]))
            got["rc", j, n] = remote(rs.at[j, n, 2], rr.at[j, n, 2], at_y(way))

    def reduce(j):
        for n in (0, 1):
            got["rc", j, n].wait_recv()
        for part, a, b in ((top, 2, 1), (low, 1, 2)):
            total = mo[j, part] + scaled_back(rr[j, 0, a]) + scaled_back(rr[j, 1, b])
            high = total.astype(BF)
            mg[j, y, part] = high
            ml[j, part] = (total - high.astype(F32)).astype(BF)
        for way in (1, -1):
            got["m", j, -way] = remote(mg.at[j, y], mg.at[j, y], at_y(way))

    def forward_merged(j, way):
        got["m", j, -way].wait_recv()
        piece = mg.at[j, wrap(y - way), top if way == 1 else low]
        got["mf", j, way] = remote(piece, piece, at_y(way))

    def add_product(left, right):
        out_ref[...] += jnp.dot(jnp.concatenate(left, axis=1), right, preferred_element_type=F32)

    def modal():
        local["q"].wait()
        for name in (("sf", 1), ("sf", -1), ("qs", 0), ("qs", 1)):
            got[name].wait_recv()
        out_ref[...] = jnp.dot(jnp.concatenate([sg[i] for i in range(G)], axis=1),
                               qg[...].reshape(G * M, RL), preferred_element_type=F32)

    def product(j):
        for way in (1, -1):
            got["mf", j, way].wait_recv()
        if j == 0:
            local["x"].wait()
        for name in list(got):
            if name[0] == "xs" and name[1] == OFFSETS[j]:
                got[name].wait_recv()
        own = pl.ds(pl.multiple_of(j * BLK + y * SUB, SUB), SUB)
        add_product([mg[j, o] for o in range(G)] + [ml[j]],
                    jnp.concatenate([xall[pl.ds(j * BLK, BLK), :], xall[own, :]], axis=0))

    def last_product():
        for way in (1, -1):
            got["mf", 3, way].wait_recv()
        last_m[...] = jnp.concatenate([mg[3, 2 - 2 * core], mg[3, 3 - 2 * core]], axis=1)
        add_product([mg[3, 2 * core], mg[3, 2 * core + 1]], xall[pl.ds(3 * BLK, ROWS), :])
        for q in (0, 2):
            got["xs", 2, q].wait_recv()

    send_coupling()
    send_modal(-1)
    send_modal(1)
    send_modal(2)
    send_coords(1, 0)
    send_scaled()
    send_coords(-1, 2)
    spread_coupling(-1)
    spread_coupling(1)
    share_own_coords()
    send_coords(1, 1)
    schur(0)
    send_coords(-1, 3)
    schur(1)
    schur(2)
    send_coords(-1, 0, 2)
    send_coords(1, 2, 2)
    share_coupling()
    combine(0)
    schur(3)
    spread_modal()
    forward_coords(1)
    combine(1)
    combine(2)
    reduce(0)
    forward_coords(-1)
    combine(3)
    reduce(1)
    reduce(2)
    reduce(3)
    forward_scaled(-1)
    forward_merged(0, -1)
    forward_merged(0, 1)
    pass_modal()
    forward_scaled(1)
    share_coords(-1, 0, False)
    forward_merged(2, -1)
    share_coords(1, 0)
    forward_merged(1, -1)
    forward_merged(2, 1)
    forward_merged(1, 1)
    forward_merged(3, 1)
    forward_merged(3, -1)
    share_coords(1, 2, False)
    share_coords(-1, 2)
    share_coords(2, 2)
    share_coords(2, 0)
    modal()
    product(0)
    product(2)
    product(1)
    last_product()
    for copy in used:
        copy.wait_send()


def on_device(interface_block, coupling, eigenvalues, mode_counts, interface_coords, modal_coords):
    held = functools.partial(pltpu.with_memory_space_constraint, memory_space=pltpu.HBM)
    hbm = pl.BlockSpec(memory_space=pltpu.HBM)
    vmem = pl.BlockSpec(memory_space=pltpu.VMEM)
    partial, merged, coords = pl.pallas_call(
        kernel,
        name="merge_recover",
        out_shape=[
            jax.ShapeDtypeStruct((ROWS, RL), F32),
            jax.ShapeDtypeStruct((ROWS, ROWS), BF),
            jax.ShapeDtypeStruct((ROWS, RL), BF),
        ],
        in_specs=[hbm] * 6,
        out_specs=[vmem] * 3,
        scratch_shapes=[
            pltpu.VMEM((1, M), F32),
            pltpu.SMEM((1,), jnp.int32),
            pltpu.VMEM((G, ROWS, BLK), F32),
            pltpu.VMEM((NI, M), BF),
            pltpu.VMEM((G, ROWS, M), BF),
            pltpu.VMEM((G, M, RL), BF),
            pltpu.VMEM((NI - ROWS, RL), BF),
            pltpu.VMEM((G, 2, 3, SUB, SUB), BF),
            pltpu.VMEM((G, 2, 3, SUB, SUB), BF),
            pltpu.VMEM((G, 2, SUB, SUB), F32),
            pltpu.VMEM((G, G, ROWS, SUB), BF),
            pltpu.VMEM((G, ROWS, SUB), F32),
            pltpu.VMEM((G, ROWS, SUB), BF),
            pltpu.SemaphoreType.DMA((COPIES,)),
            pltpu.SemaphoreType.DMA((COPIES,)),
            pltpu.SemaphoreType.DMA((9,)),
        ],
        compiler_params=pltpu.CompilerParams(
            collective_id=0, has_side_effects=True, vmem_limit_bytes=40 * 2**20),
        cost_estimate=pl.CostEstimate(flops=1_500_000_000, bytes_accessed=5 * 2**20, transcendentals=0),
    )(held(interface_block), held(coupling), held(eigenvalues), mode_counts, held(interface_coords), held(modal_coords))
    return (partial + jnp.dot(merged, coords, preferred_element_type=F32))[None]


def solution(mesh):
    placed = (
        P("leaf", "panel", None),
        P("leaf", "panel", None),
        P("leaf", None),
        P("leaf"),
        P("leaf", "panel", None),
        P("leaf", None, None),
    )
    return jax.shard_map(
        on_device, mesh=mesh, in_specs=placed, out_specs=P("leaf", "panel", None), check_vma=False
    )
```
